32 devices in a mesh: section: 4 (over y, core), expert: 8 (over z, x).
Axes of the slice: x: 2, y: 2, z: 4, core: 2. Of those that a mesh axis runs over, the one named last changes fastest.
Arguments:
- acts_fwd: bfloat16 [4, 1024, 7168], P('section', 'expert'), may hold values from -6 to 6
- routes_fwd: int32 [4, 1024, 1], P('section', 'expert'), may hold values from 0 to 1; in each aligned block of 128 rows (0 to 127, 128 to 255, ..., all dimensions but the last counted through in order) at most 72 rows name the same one
- gates_fwd: float32 [4, 1024, 1], P('section', 'expert'), may hold values from 0.2 to 1.5
- stash_bwd: bfloat16 [4, 1024, 7168], P('section', 'expert'), may hold values from -6 to 6
- grads_bwd: bfloat16 [4, 1024, 7168], P('section', 'expert'), may hold values from -6 to 6
- routes_bwd: int32 [4, 1024, 1], P('section', 'expert'), may hold values from 0 to 1; in each aligned block of 128 rows (0 to 127, 128 to 255, ..., all dimensions but the last counted through in order) at most 72 rows name the same one
- gates_bwd: float32 [4, 1024, 1], P('section', 'expert'), may hold values from 0.2 to 1.5
- gain: float32 [4, 7168], P('section'), may hold values from 0.1 to 1.9
- w_gate: bfloat16 [4, 7168, 2048], P('section', None, 'expert'), may hold values from -0.0625 to 0.0625
- w_up: bfloat16 [4, 7168, 2048], P('section', None, 'expert'), may hold values from -0.0625 to 0.0625
- w_down: bfloat16 [4, 2048, 7168], P('section', 'expert'), may hold values from -0.1875 to 0.1875
Outputs:
- fwd_next: bfloat16 [4, 1024, 7168], P('section', 'expert')
- grad_next: bfloat16 [4, 1024, 7168], P('section', 'expert')
The draws below stay inside these ranges and needn't reach their ends.
Inputs may be any that keep to these rules, and one draw needn't show every extreme that they name: `routes_fwd`: each row names 1 different experts. In the rows of one device (aligned blocks of 128 rows of one layer) no expert is named by more than 72 rows, a bound that some block reaches. `routes_bwd`: each row names 1 different experts. In the rows of one device (aligned blocks of 128 rows of one layer) no expert is named by more than 72 rows, a bound that some block reaches.
All inputs are finite; a program needn't handle non-finite values.
Results may differ from the reference program's by a relative error of at most 0.006.
Values may be sent and summed in bfloat16 or wider, within the bound.
A program may use at most 128 MiB of HBM per device.

```python
import math
import jax
import jax.numpy as jnp
import numpy as np
from jax import lax

D = 7168
FFW = 1024
SHARDS = 4
TOP = 1
TOK_DEV = 128
SECTIONS = 4
EXPERTS = 2
TOKENS = 1024
CAP = 72
N_EXPERT = 8


def levels(own_key, shape, pieces, smallest, largest):
    level, own = 1.0, jax.random.fold_in(own_key, 6)
    for position, parts in pieces:
        draws = jnp.exp(jax.random.uniform(jax.random.fold_in(own, position), (parts,), jnp.float32, smallest / len(pieces), largest / len(pieces)))
        level = level * jnp.repeat(draws, shape[position] // parts).reshape([-1 if axis == position else 1 for axis in range(len(shape))])
    return level


def deal_out(rng, own, number, rows, count, top, reach, lean):
    order = jax.random.permutation(rng, count)
    packed, usual = shares(count, rows * top, reach, lean, True), shares(count, rows * top, reach, lean, False)
    places = jnp.arange(count)

    def named(sizes, offset_by):
        used = int((sizes > 0).sum())
        fixed = max(1, used // 4)
        shifted = fixed + (places - fixed + offset_by * (used - fixed)) % max(1, count - fixed)
        return jnp.zeros((count,), jnp.int32).at[order[jnp.where(places < fixed, places, shifted)]].set(jnp.asarray(sizes, jnp.int32))

    sizes = jnp.where(number % 4 == 0, named(packed, number // 4), named(usual, number - number // 4 - 1))
    mixed = jax.random.permutation(jax.random.fold_in(own, 3), count)
    source_of, sink = mixed[0:count // 2 * 2:2], mixed[1:count // 2 * 2:2]
    room = jnp.minimum(sizes[source_of] - 1, reach - sizes[sink]) // 2
    room = jnp.where((source_of == order[0]) | (sink == order[0]) | (sizes[sink] == 0), 0, jnp.maximum(room, 0))
    shifted = jax.random.randint(jax.random.fold_in(own, 4), (count // 2,), 0, 1 << 20) % (room + 1)
    sizes = sizes.at[source_of].add(-shifted).at[sink].add(shifted)
    labels = jnp.searchsorted(jnp.cumsum(sizes), jnp.arange(rows * top), side="right").astype(jnp.int32)
    listing = labels.reshape(top, rows).T
    listing = listing[jax.random.permutation(jax.random.fold_in(own, 1), rows)]
    offset_by = jax.random.randint(jax.random.fold_in(own, 2), (rows, 1), 0, top)
    return jnp.take_along_axis(listing, (jnp.arange(top)[None, :] + offset_by) % top, axis=1)


def shares(number_of, total, limit, slope, full):
    weights = [(1 << 20) // math.isqrt(rank ** slope) + 1 for rank in range(1, number_of + 1)]
    largest = limit if full else min(limit, max(-(-total // number_of), total * weights[0] // sum(weights)))
    least = 1 if total - largest >= number_of - 1 else 0
    counts, rest = [largest] + [least] * (number_of - 1), total - largest - least * (number_of - 1)
    while rest > 0:
        movable = [i for i in range(1, number_of) if counts[i] < largest] or [i for i in range(1, number_of) if counts[i] < limit]
        mass, remaining = sum([weights[i] for i in movable]), rest
        for i in movable:
            extra = min(limit - counts[i], max(1, remaining * weights[i] // mass), rest)
            counts[i] = counts[i] + extra
            rest = rest - extra
    return np.array(counts)


def bell_draw(own_key, extent, deviation, most, split=(), kind=jnp.bfloat16):
    level = levels(own_key, extent, split, -0.22, 0.18) if split else 1.0
    drawn = jax.random.normal(own_key, extent, jnp.float32) * deviation * level
    return jnp.minimum(jnp.maximum(drawn, -most), most).astype(kind)


def setup_inputs(seed: int = 0) -> dict:
    splits = jax.random.split(jax.random.key(seed), 12)
    acts_fwd = bell_draw(splits[0], (SECTIONS, TOKENS, D), 1.0, 6.0, ((0, 4), (1, 8)))
    routes_fwd_keys = jax.random.split(jax.random.fold_in(splits[1], 1), SECTIONS * TOKENS // TOK_DEV)
    routes_fwd_turns = jax.random.permutation(jax.random.fold_in(splits[1], 3), SECTIONS * TOKENS // TOK_DEV)
    routes_fwd = jax.vmap(lambda own, number: deal_out(jax.random.fold_in(splits[1], 2), own, number, TOK_DEV, EXPERTS, TOP, CAP, 2))(routes_fwd_keys, routes_fwd_turns).reshape((SECTIONS, TOKENS, TOP))
    gates_fwd = jnp.clip(jnp.exp(math.log(1.5) - 2.014903 * jax.random.uniform(splits[2], (SECTIONS, TOKENS, TOP), jnp.float32) ** levels(splits[2], (SECTIONS, TOKENS, TOP), ((0, 4), (1, 8)), -0.2, 0.2)), 0.2, 1.5)
    stash_bwd = bell_draw(splits[3], (SECTIONS, TOKENS, D), 1.0, 6.0, ((0, 4), (1, 8)))
    grads_bwd = bell_draw(splits[4], (SECTIONS, TOKENS, D), 1.0, 6.0, ((0, 4), (1, 8)))
    routes_bwd_keys = jax.random.split(jax.random.fold_in(splits[5], 1), SECTIONS * TOKENS // TOK_DEV)
    routes_bwd_turns = jax.random.permutation(jax.random.fold_in(splits[5], 3), SECTIONS * TOKENS // TOK_DEV)
    routes_bwd = jax.vmap(lambda own, number: deal_out(jax.random.fold_in(splits[5], 2), own, number, TOK_DEV, EXPERTS, TOP, CAP, 2))(routes_bwd_keys, routes_bwd_turns).reshape((SECTIONS, TOKENS, TOP))
    gates_bwd = jnp.clip(jnp.exp(math.log(1.5) - 2.014903 * jax.random.uniform(splits[6], (SECTIONS, TOKENS, TOP), jnp.float32) ** levels(splits[6], (SECTIONS, TOKENS, TOP), ((0, 4), (1, 8)), -0.2, 0.2)), 0.2, 1.5)
    gain = jnp.clip(1.0 + 0.18 * jax.random.normal(splits[7], (SECTIONS, D), jnp.float32), 0.1, 1.9)
    w_gate = bell_draw(splits[8], (SECTIONS, D, EXPERTS * FFW), D ** -0.5, 0.0625, ((0, 4), (2, 8)))
    w_up = bell_draw(splits[9], (SECTIONS, D, EXPERTS * FFW), D ** -0.5, 0.0625, ((0, 4), (2, 8)))
    w_down = bell_draw(splits[10], (SECTIONS, EXPERTS * FFW, D), FFW ** -0.5, 0.1875, ((0, 4), (1, 8)))
    return dict(acts_fwd=acts_fwd, routes_fwd=routes_fwd, gates_fwd=gates_fwd, stash_bwd=stash_bwd, grads_bwd=grads_bwd, routes_bwd=routes_bwd, gates_bwd=gates_bwd, gain=gain, w_gate=w_gate, w_up=w_up, w_down=w_down)


EPS = 1e-06
PRECISE = lax.Precision.HIGHEST

def normed(token_rows, gain_row):
    values = token_rows.astype(jnp.float32)
    factor = lax.rsqrt(lax.optimization_barrier(jnp.mean(values * values, axis=-1, keepdims=True)) + EPS)
    return values * factor * gain_row

def tables(route_ids, gate_vals, experts_n, capacity):
    flat_ids = route_ids.reshape(-1)
    one_hot = (flat_ids[:, None] == jnp.arange(experts_n, dtype=jnp.int32)[None, :]).astype(jnp.int32)
    slot_ids = lax.optimization_barrier(jnp.sum((jnp.cumsum(one_hot, axis=0) - one_hot) * one_hot, axis=1)).reshape(route_ids.shape)
    expert_hit = route_ids[None] == jnp.arange(experts_n, dtype=jnp.int32)[:, None, None]
    slot_hit = slot_ids[None] == jnp.arange(capacity, dtype=jnp.int32)[:, None, None]
    placed = expert_hit[:, None] & slot_hit[None]
    select = lax.optimization_barrier(jnp.sum(placed.astype(jnp.float32), axis=-1))
    weighted = lax.optimization_barrier(jnp.sum(jnp.where(placed, gate_vals[None, None], jnp.float32(0.0)), axis=-1))
    return (select, weighted)

def pack_rows(select, token_rows):
    return jnp.einsum('ect,td->ecd', select.astype(jnp.bfloat16), token_rows, preferred_element_type=jnp.float32).astype(jnp.bfloat16)

def pack_scaled(weighted, token_rows):
    return jnp.einsum('ect,td->ecd', weighted, token_rows.astype(jnp.float32), precision=PRECISE).astype(jnp.bfloat16)

def expert_forward(token_rows, gate_cols, up_cols, down_rows):
    pre_gate = jnp.dot(token_rows, gate_cols, preferred_element_type=jnp.float32)
    pre_up = jnp.dot(token_rows, up_cols, preferred_element_type=jnp.float32)
    hidden = (pre_gate * jax.nn.sigmoid(pre_gate) * pre_up).astype(jnp.bfloat16)
    width = FFW // SHARDS
    total = jnp.zeros((token_rows.shape[0], D), jnp.float32)
    for shard in range(SHARDS):
        piece = jnp.dot(hidden[:, shard * width:(shard + 1) * width], down_rows[shard * width:(shard + 1) * width], preferred_element_type=jnp.float32)
        total = total + piece.astype(jnp.bfloat16).astype(jnp.float32)
    return total

def expert_backward(token_rows, upstream, gate_cols, up_cols, down_rows):
    pre_gate = jnp.dot(token_rows, gate_cols, preferred_element_type=jnp.float32)
    pre_up = jnp.dot(token_rows, up_cols, preferred_element_type=jnp.float32)
    contract = (((1,), (1,)), ((), ()))
    grad_hidden = lax.dot_general(upstream, down_rows, contract, preferred_element_type=jnp.float32)
    sigmoid_gate = jax.nn.sigmoid(pre_gate)
    grad_gate = (grad_hidden * pre_up * sigmoid_gate * (1.0 + pre_gate * (1.0 - sigmoid_gate))).astype(jnp.bfloat16)
    grad_up = (grad_hidden * pre_gate * sigmoid_gate).astype(jnp.bfloat16)
    width = FFW // SHARDS
    total = jnp.zeros((token_rows.shape[0], D), jnp.float32)
    for shard in range(SHARDS):
        low = shard * width
        high = low + width
        first = lax.dot_general(grad_gate[:, low:high], gate_cols[:, low:high], contract, preferred_element_type=jnp.float32)
        second = lax.dot_general(grad_up[:, low:high], up_cols[:, low:high], contract, preferred_element_type=jnp.float32)
        total = total + (first + second).astype(jnp.bfloat16).astype(jnp.float32)
    return total

def split_experts(gate_all, up_all, down_all):
    gate_each = gate_all.reshape(D, EXPERTS, FFW).transpose(1, 0, 2)
    up_each = up_all.reshape(D, EXPERTS, FFW).transpose(1, 0, 2)
    down_each = down_all.reshape(EXPERTS, FFW, D)
    return (gate_each, up_each, down_each)

def to_experts(sent_rows):
    return sent_rows.transpose(1, 0, 2, 3).reshape(EXPERTS, N_EXPERT * CAP, D)

def from_experts(partials):
    return partials.reshape(EXPERTS, N_EXPERT, CAP, D).transpose(1, 0, 2, 3)

def route_tables(route_ids, gate_vals):

    def one_block(block_ids, block_gates):
        return tables(block_ids, block_gates, EXPERTS, CAP)
    return jax.vmap(one_block)(route_ids.reshape(N_EXPERT, TOK_DEV, TOP), gate_vals.reshape(N_EXPERT, TOK_DEV, TOP))

def forward_layer(acts, route_ids, gate_vals, gain_row, gate_all, up_all, down_all):
    gate_each, up_each, down_each = split_experts(gate_all, up_all, down_all)
    normed_rows = normed(acts, gain_row).astype(jnp.bfloat16).reshape(N_EXPERT, TOK_DEV, D)
    select, weighted = route_tables(route_ids, gate_vals)
    sent_rows = to_experts(jax.vmap(pack_rows)(select, normed_rows))

    def one_expert(operands):
        return expert_forward(operands[0], operands[1], operands[2], operands[3])
    partials = from_experts(lax.map(one_expert, (sent_rows, gate_each, up_each, down_each)))
    mixture = jnp.einsum('nect,necd->ntd', weighted, partials, precision=PRECISE).reshape(TOKENS, D)
    return (acts.astype(jnp.float32) + mixture).astype(jnp.bfloat16)

def backward_layer(stashed, grads, route_ids, gate_vals, gain_row, gate_all, up_all, down_all):
    gate_each, up_each, down_each = split_experts(gate_all, up_all, down_all)
    normed_rows = normed(stashed, gain_row).astype(jnp.bfloat16).reshape(N_EXPERT, TOK_DEV, D)
    select, weighted = route_tables(route_ids, gate_vals)
    sent_rows = to_experts(jax.vmap(pack_rows)(select, normed_rows))
    sent_grads = to_experts(jax.vmap(pack_scaled)(weighted, grads.reshape(N_EXPERT, TOK_DEV, D)))

    def one_expert(operands):
        return expert_backward(operands[0], operands[1], operands[2], operands[3], operands[4])
    partials = from_experts(lax.map(one_expert, (sent_rows, sent_grads, gate_each, up_each, down_each)))
    grad_normed = jnp.einsum('nect,necd->ntd', select, partials, precision=PRECISE).reshape(TOKENS, D)

    def norm_only(values):
        return normed(values, gain_row)
    unused, pullback = jax.vjp(norm_only, stashed.astype(jnp.float32))
    return (grads.astype(jnp.float32) + pullback(grad_normed)[0]).astype(jnp.bfloat16)

def reference(acts_fwd, routes_fwd, gates_fwd, stash_bwd, grads_bwd, routes_bwd, gates_bwd, gain, w_gate, w_up, w_down):
    outputs = []
    gradients = []
    for layer_idx in range(SECTIONS):
        outputs.append(forward_layer(acts_fwd[layer_idx], routes_fwd[layer_idx], gates_fwd[layer_idx], gain[layer_idx], w_gate[layer_idx], w_up[layer_idx], w_down[layer_idx]))
        gradients.append(backward_layer(stash_bwd[layer_idx], grads_bwd[layer_idx], routes_bwd[layer_idx], gates_bwd[layer_idx], gain[layer_idx], w_gate[layer_idx], w_up[layer_idx], w_down[layer_idx]))
    layer_out = jnp.stack(outputs)
    grad_input = jnp.stack(gradients)
    return (jnp.roll(layer_out, 1, axis=0), jnp.roll(grad_input, -1, axis=0))
```

```python
import jax
import jax.numpy as jnp
from jax import lax
from jax.sharding import PartitionSpec as P

SHARDS = 4
TOP = 1


EPS = 1e-06


def from_behind(value, axis, by):
    devices = lax.axis_size(axis)
    return lax.ppermute(value, axis, [(i, (i + by) % devices) for i in range(devices)])


def normed(token_rows, gain_row):
    values = token_rows.astype(jnp.float32)
    factor = lax.rsqrt(jnp.mean(values * values, axis=-1, keepdims=True) + EPS)
    return values * factor * gain_row


def slot_tables(route_ids, gate_vals, experts_n, capacity):
    tok_rows, top_n = route_ids.shape
    flat_ids = route_ids.reshape(-1)
    one_hot = (flat_ids[:, None] == jnp.arange(experts_n, dtype=jnp.int32)[None, :]).astype(
        jnp.int32
    )
    slot_ids = jnp.sum((jnp.cumsum(one_hot, axis=0) - one_hot) * one_hot, axis=1)
    position = flat_ids * capacity + slot_ids
    places = jnp.arange(experts_n * capacity, dtype=jnp.int32)
    hit = position[None, :] == places[:, None]
    slot_gate = jnp.sum(jnp.where(hit, gate_vals.reshape(-1)[None, :], jnp.float32(0.0)), axis=1)
    select = jnp.sum(hit.reshape(-1, tok_rows, top_n), axis=2).astype(jnp.bfloat16)
    return select, slot_gate


def pick(select, rows):
    return jnp.dot(select, rows, preferred_element_type=jnp.float32)


def expert_forward(token_rows, gate_cols, up_cols, down_rows):
    pre_gate = jnp.dot(token_rows, gate_cols, preferred_element_type=jnp.float32)
    pre_up = jnp.dot(token_rows, up_cols, preferred_element_type=jnp.float32)
    hidden = (pre_gate * jax.nn.sigmoid(pre_gate) * pre_up).astype(jnp.bfloat16)
    return jnp.dot(hidden, down_rows, preferred_element_type=jnp.float32)


def expert_backward(token_rows, upstream, gate_cols, up_cols, down_rows):
    pre_gate = jnp.dot(token_rows, gate_cols, preferred_element_type=jnp.float32)
    pre_up = jnp.dot(token_rows, up_cols, preferred_element_type=jnp.float32)
    contract = (((1,), (1,)), ((), ()))
    grad_hidden = lax.dot_general(upstream, down_rows, contract, preferred_element_type=jnp.float32)
    sigmoid_gate = jax.nn.sigmoid(pre_gate)
    grad_gate = (
        grad_hidden * pre_up * sigmoid_gate * (1.0 + pre_gate * (1.0 - sigmoid_gate))
    ).astype(jnp.bfloat16)
    grad_up = (grad_hidden * pre_gate * sigmoid_gate).astype(jnp.bfloat16)
    first = lax.dot_general(grad_gate, gate_cols, contract, preferred_element_type=jnp.float32)
    second = lax.dot_general(grad_up, up_cols, contract, preferred_element_type=jnp.float32)
    return first + second


def local(
    acts_fwd,
    routes_fwd,
    gates_fwd,
    stash_bwd,
    grads_bwd,
    routes_bwd,
    gates_bwd,
    gain,
    w_gate,
    w_up,
    w_down,
):
    devices = lax.axis_size("expert")
    experts_n = devices // SHARDS
    tok_rows, features = acts_fwd.shape[1:]
    capacity = min(tok_rows, 9 * tok_rows * TOP // (8 * experts_n))
    gate_cols = w_gate[0]
    up_cols = w_up[0]
    down_rows = w_down[0]
    gain_row = gain[0]
    across = [[e * SHARDS + s for e in range(experts_n)] for s in range(SHARDS)]
    within = [[e * SHARDS + s for s in range(SHARDS)] for e in range(experts_n)]

    def outward(packed):
        swapped = lax.all_to_all(
            packed, "expert", 0, 0, axis_index_groups=across, tiled=True
        )
        return lax.all_gather(swapped, "expert", axis_index_groups=within, axis=0, tiled=True)

    def back(result):
        summed = lax.psum_scatter(
            result, "expert", scatter_dimension=0, axis_index_groups=within, tiled=True
        )
        return lax.all_to_all(summed, "expert", 0, 0, axis_index_groups=across, tiled=True)

    entering = acts_fwd[0]
    select_fwd, unused_gate = slot_tables(routes_fwd[0], gates_fwd[0], experts_n, capacity)
    rows_fwd = pick(select_fwd, normed(entering, gain_row).astype(jnp.bfloat16)).astype(jnp.bfloat16)
    stashed = stash_bwd[0]
    upstream = grads_bwd[0]
    select_bwd, slot_gate = slot_tables(routes_bwd[0], gates_bwd[0], experts_n, capacity)
    rows_bwd = pick(select_bwd, normed(stashed, gain_row).astype(jnp.bfloat16)).astype(jnp.bfloat16)
    rows_grad = (pick(select_bwd, upstream) * slot_gate[:, None]).astype(jnp.bfloat16)
    all_fwd = outward(rows_fwd)
    all_bwd = outward(rows_bwd)
    all_grad = outward(rows_grad)
    result = expert_forward(all_fwd, gate_cols, up_cols, down_rows).astype(jnp.bfloat16)
    back_fwd = back(result)
    result = expert_backward(all_bwd, all_grad, gate_cols, up_cols, down_rows).astype(jnp.bfloat16)
    back_bwd = back(result)
    mixture = gates_fwd[0] * pick(select_fwd.T, back_fwd)
    layer_out = (entering.astype(jnp.float32) + mixture).astype(jnp.bfloat16)
    grad_normed = pick(select_bwd.T, back_bwd)

    def norm_only(values):
        return normed(values, gain_row)

    unused, pullback = jax.vjp(norm_only, stashed.astype(jnp.float32))
    grad_input = (upstream.astype(jnp.float32) + pullback(grad_normed)[0]).astype(jnp.bfloat16)
    fwd_next = from_behind(layer_out[None], "section", 1)
    grad_next = from_behind(grad_input[None], "section", -1)
    return (fwd_next, grad_next)


def solution(mesh):
    return jax.shard_map(
        local,
        mesh=mesh,
        in_specs=(
            P("section", "expert", None),
            P("section", "expert", None),
            P("section", "expert", None),
            P("section", "expert", None),
            P("section", "expert", None),
            P("section", "expert", None),
            P("section", "expert", None),
            P("section", None),
            P("section", None, "expert"),
            P("section", None, "expert"),
            P("section", "expert", None),
        ),
        out_specs=(P("section", "expert", None), P("section", "expert", None)),
        check_vma=False,
    )
```

```python
import functools

import jax
import jax.numpy as jnp
from jax import lax
from jax.experimental import pallas as pl
from jax.experimental.pallas import tpu as pltpu
from jax.sharding import PartitionSpec as P

SHARDS = 4
TOP = 1


EPS = 1e-06


def from_behind(value, axis, by):
    devices = lax.axis_size(axis)
    return lax.ppermute(value, axis, [(i, (i + by) % devices) for i in range(devices)])


def normed(token_rows, gain_row):
    values = token_rows.astype(jnp.float32)
    factor = lax.rsqrt(jnp.mean(values * values, axis=-1, keepdims=True) + EPS)
    return values * factor * gain_row


def slot_tables(route_ids, gate_vals, experts_n, capacity):
    tok_rows, top_n = route_ids.shape
    flat_ids = route_ids.reshape(-1)
    one_hot = (flat_ids[:, None] == jnp.arange(experts_n, dtype=jnp.int32)[None, :]).astype(
        jnp.int32
    )
    slot_ids = jnp.sum((jnp.cumsum(one_hot, axis=0) - one_hot) * one_hot, axis=1)
    position = flat_ids * capacity + slot_ids
    places = jnp.arange(experts_n * capacity, dtype=jnp.int32)
    hit = position[None, :] == places[:, None]
    slot_gate = jnp.sum(jnp.where(hit, gate_vals.reshape(-1)[None, :], jnp.float32(0.0)), axis=1)
    select = jnp.sum(hit.reshape(-1, tok_rows, top_n), axis=2).astype(jnp.bfloat16)
    return select, slot_gate


def pick(select, rows):
    return jnp.dot(select, rows, preferred_element_type=jnp.float32)


def expert_forward(token_rows, gate_cols, up_cols, down_rows):
    pre_gate = jnp.dot(token_rows, gate_cols, preferred_element_type=jnp.float32)
    pre_up = jnp.dot(token_rows, up_cols, preferred_element_type=jnp.float32)
    hidden = (pre_gate * jax.nn.sigmoid(pre_gate) * pre_up).astype(jnp.bfloat16)
    return jnp.dot(hidden, down_rows, preferred_element_type=jnp.float32)


def expert_backward(token_rows, upstream, gate_cols, up_cols, down_rows):
    pre_gate = jnp.dot(token_rows, gate_cols, preferred_element_type=jnp.float32)
    pre_up = jnp.dot(token_rows, up_cols, preferred_element_type=jnp.float32)
    contract = (((1,), (1,)), ((), ()))
    grad_hidden = lax.dot_general(upstream, down_rows, contract, preferred_element_type=jnp.float32)
    sigmoid_gate = jax.nn.sigmoid(pre_gate)
    grad_gate = (
        grad_hidden * pre_up * sigmoid_gate * (1.0 + pre_gate * (1.0 - sigmoid_gate))
    ).astype(jnp.bfloat16)
    grad_up = (grad_hidden * pre_gate * sigmoid_gate).astype(jnp.bfloat16)
    first = lax.dot_general(grad_gate, gate_cols, contract, preferred_element_type=jnp.float32)
    second = lax.dot_general(grad_up, up_cols, contract, preferred_element_type=jnp.float32)
    return first + second


MESH = pl.DeviceIdType.MESH
VMEM_BYTES = 58 * 1024 * 1024


def swap_last(position):
    return position + (position // 2) * (1 - 2 * (position % 2))


def ring_shard(position, experts_n):
    position = position % SHARDS
    return swap_last(position) if experts_n == 2 else position


def places(experts_n):
    me = lax.axis_index("expert")
    group, shard = me // SHARDS, me % SHARDS
    position = swap_last(shard) if experts_n == 2 else shard
    right = ring_shard(position + 1, experts_n)
    far = ring_shard(position + 2, experts_n)
    left = ring_shard(position + 3, experts_n)
    return group, shard, left, right, far


def greet(experts_n, group, shard, left, right):
    barrier = pltpu.get_barrier_semaphore()
    partners = [group * SHARDS + left, group * SHARDS + right]
    for step in range(1, experts_n):
        partners.append((group + step) % experts_n * SHARDS + shard)
    for partner in partners:
        pl.semaphore_signal(barrier, inc=1, device_id={"expert": partner}, device_id_type=MESH)
    pl.semaphore_wait(barrier, len(partners))


def remote(src, dst, send, recv, target):
    return pltpu.make_async_remote_copy(
        src_ref=src,
        dst_ref=dst,
        send_sem=send,
        recv_sem=recv,
        device_id={"expert": target},
        device_id_type=MESH,
    )


def outward_kernel(experts_n, arrays, *refs):
    packed, gathered = refs[:arrays], refs[arrays : 2 * arrays]
    cross_send, cross_recv, ring_send, ring_recv, half_send, half_recv, local_sem = refs[2 * arrays :]
    group, shard, left, right, far = places(experts_n)
    greet(experts_n, group, shard, left, right)
    half = packed[0].shape[2] // 2
    sides = ((right, left), (left, right))
    started = []

    def begin(copy):
        copy.start()
        started.append(copy)
        return copy

    crossing, ring, local = {}, {}, []
    for a in range(arrays):
        for step in range(1, experts_n):
            expert = (group + step) % experts_n
            crossing[a, step] = begin(
                remote(
                    packed[a].at[expert],
                    gathered[a].at[group, shard],
                    cross_send.at[a, step],
                    cross_recv.at[a, step],
                    expert * SHARDS + shard,
                )
            )
        for side, (target, unused) in enumerate(sides):
            ring[a, 0, side] = begin(
                remote(
                    packed[a].at[group],
                    gathered[a].at[group, shard],
                    ring_send.at[a, 0, side],
                    ring_recv.at[a, 0, side],
                    group * SHARDS + target,
                )
            )
        copy = pltpu.make_async_copy(
            packed[a].at[group], gathered[a].at[group, shard], local_sem.at[a]
        )
        copy.start()
        local.append(copy)

    def relay(a, step):
        origin = (group + experts_n - step) % experts_n
        for side, (target, source) in enumerate(sides):
            ring[a, step, side].wait_recv()
            block = gathered[a].at[origin, source, :, pl.ds(side * half, half)]
            halves[a, step, side] = begin(
                remote(
                    block,
                    block,
                    half_send.at[a, step, side],
                    half_recv.at[a, step, side],
                    group * SHARDS + target,
                )
            )

    halves = {}
    for a in range(arrays):
        for step in range(1, experts_n):
            origin = (group + experts_n - step) % experts_n
            crossing[a, step].wait_recv()
            block = gathered[a].at[origin, shard]
            for side, (target, unused) in enumerate(sides):
                ring[a, step, side] = begin(
                    remote(
                        block,
                        block,
                        ring_send.at[a, step, side],
                        ring_recv.at[a, step, side],
                        group * SHARDS + target,
                    )
                )
        relay(a, 0)
        if a > 0:
            for step in range(1, experts_n):
                relay(a - 1, step)
    for step in range(1, experts_n):
        relay(arrays - 1, step)
    for copy in halves.values():
        copy.wait_recv()
    for copy in local:
        copy.wait()
    for copy in started:
        copy.wait_send()


def outward_call(packed, experts_n):
    arrays = len(packed)
    unused, capacity, features = packed[0].shape
    dma = pltpu.SemaphoreType.DMA
    shape = jax.ShapeDtypeStruct((experts_n, SHARDS, capacity, features), jnp.bfloat16)
    return pl.pallas_call(
        functools.partial(outward_kernel, experts_n, arrays),
        out_shape=[shape] * arrays,
        in_specs=[pl.BlockSpec(memory_space=pl.ANY)] * arrays,
        out_specs=[pl.BlockSpec(memory_space=pl.ANY)] * arrays,
        scratch_shapes=[
            dma((arrays, experts_n)),
            dma((arrays, experts_n)),
            dma((arrays, experts_n, 2)),
            dma((arrays, experts_n, 2)),
            dma((arrays, experts_n, 2)),
            dma((arrays, experts_n, 2)),
            dma((arrays,)),
        ],
        compiler_params=pltpu.CompilerParams(
            collective_id=0, has_side_effects=True, vmem_limit_bytes=VMEM_BYTES
        ),
        name="rows_to_experts",
    )(*packed)


def add_into(dst, terms, columns):
    tile = 512 if columns % 512 == 0 else 128

    @pl.loop(0, columns // tile)
    def _(i):
        at = pl.ds(pl.multiple_of(i * tile, tile), tile)
        total = terms[0][:, at].astype(jnp.float32)
        for term in terms[1:]:
            total = total + term[:, at].astype(jnp.float32)
        dst[:, at] = total.astype(dst.dtype)


def return_kernel(experts_n, arrays, *refs):
    partial, summed = refs[:arrays], refs[arrays : 2 * arrays]
    far_in, near_in, total, far_send, far_recv, near_send, near_recv, out_send, out_recv, local_sem = refs[
        2 * arrays :
    ]
    group, shard, left, right, far = places(experts_n)
    greet(experts_n, group, shard, left, right)
    half = partial[0].shape[3] // 2
    sides = ((right, left), (left, right))
    cols = (pl.ds(0, half), pl.ds(half, half))
    started, far_copies, near_copies, out_copies, local = [], {}, {}, {}, []

    def begin(copy):
        copy.start()
        started.append(copy)
        return copy

    order = [(a, step) for a in range(arrays) for step in list(range(1, experts_n)) + [0]]
    for a, step in order:
        origin = (group + step) % experts_n
        for side, (target, unused) in enumerate(sides):
            far_copies[a, step, side] = begin(
                remote(
                    partial[a].at[origin, far, :, cols[side]],
                    far_in.at[a, step, side],
                    far_send.at[a, step, side],
                    far_recv.at[a, step, side],
                    group * SHARDS + target,
                )
            )
    for a, step in order:
        origin = (group + step) % experts_n
        for side, (target, unused) in enumerate(sides):
            near_copies[a, step, side, 1] = begin(
                remote(
                    partial[a].at[origin, target, :, cols[1 - side]],
                    near_in.at[a, step, side, :, cols[1 - side]],
                    near_send.at[a, step, side, 1],
                    near_recv.at[a, step, side, 1],
                    group * SHARDS + target,
                )
            )
    for a, step in order:
        origin = (group + step) % experts_n
        for side, (target, unused) in enumerate(sides):
            far_copies[a, step, side].wait_recv()
            block = far_in.at[a, step, side]
            add_into(block, (block, partial[a].at[origin, target, :, cols[side]]), half)
            near_copies[a, step, side, 0] = begin(
                remote(
                    block,
                    near_in.at[a, step, side, :, cols[side]],
                    near_send.at[a, step, side, 0],
                    near_recv.at[a, step, side, 0],
                    group * SHARDS + target,
                )
            )
    for a, step in order:
        origin = (group + step) % experts_n
        for side in range(2):
            for part in range(2):
                near_copies[a, step, side, part].wait_recv()
        result = total.at[a, step]
        add_into(
            result,
            (near_in.at[a, step, 0], near_in.at[a, step, 1], partial[a].at[origin, shard]),
            2 * half,
        )
        if step == 0:
            copy = pltpu.make_async_copy(result, summed[a].at[group], local_sem.at[a])
            copy.start()
            local.append(copy)
        else:
            out_copies[a, step] = begin(
                remote(
                    result,
                    summed[a].at[group],
                    out_send.at[a, step],
                    out_recv.at[a, step],
                    origin * SHARDS + shard,
                )
            )
    for copy in out_copies.values():
        copy.wait_recv()
    for copy in local:
        copy.wait()
    for copy in started:
        copy.wait_send()


def return_call(partial):
    arrays = len(partial)
    experts_n, unused, capacity, features = partial[0].shape
    dma = pltpu.SemaphoreType.DMA
    shape = jax.ShapeDtypeStruct((experts_n, capacity, features), jnp.bfloat16)
    return pl.pallas_call(
        functools.partial(return_kernel, experts_n, arrays),
        out_shape=[shape] * arrays,
        in_specs=[pl.BlockSpec(memory_space=pltpu.VMEM)] * arrays,
        out_specs=[pl.BlockSpec(memory_space=pl.ANY)] * arrays,
        scratch_shapes=[
            pltpu.VMEM((arrays, experts_n, 2, capacity, features // 2), jnp.bfloat16),
            pltpu.VMEM((arrays, experts_n, 2, capacity, features), jnp.bfloat16),
            pltpu.VMEM((arrays, experts_n, capacity, features), jnp.bfloat16),
            dma((arrays, experts_n, 2)),
            dma((arrays, experts_n, 2)),
            dma((arrays, experts_n, 2, 2)),
            dma((arrays, experts_n, 2, 2)),
            dma((arrays, experts_n)),
            dma((arrays, experts_n)),
            dma((arrays,)),
        ],
        compiler_params=pltpu.CompilerParams(
            collective_id=1, has_side_effects=True, vmem_limit_bytes=VMEM_BYTES
        ),
        name="sums_to_tokens",
    )(*partial)


def local(
    acts_fwd,
    routes_fwd,
    gates_fwd,
    stash_bwd,
    grads_bwd,
    routes_bwd,
    gates_bwd,
    gain,
    w_gate,
    w_up,
    w_down,
):
    devices = lax.axis_size("expert")
    experts_n = devices // SHARDS
    tok_rows, features = acts_fwd.shape[1:]
    capacity = min(tok_rows, 9 * tok_rows * TOP // (8 * experts_n))
    gate_cols = w_gate[0]
    up_cols = w_up[0]
    down_rows = w_down[0]
    gain_row = gain[0]
    entering = acts_fwd[0]
    select_fwd, unused_gate = slot_tables(routes_fwd[0], gates_fwd[0], experts_n, capacity)
    rows_fwd = pick(select_fwd, normed(entering, gain_row).astype(jnp.bfloat16)).astype(jnp.bfloat16)
    stashed = stash_bwd[0]
    upstream = grads_bwd[0]
    select_bwd, slot_gate = slot_tables(routes_bwd[0], gates_bwd[0], experts_n, capacity)
    rows_bwd = pick(select_bwd, normed(stashed, gain_row).astype(jnp.bfloat16)).astype(jnp.bfloat16)
    rows_grad = (pick(select_bwd, upstream) * slot_gate[:, None]).astype(jnp.bfloat16)
    packed = [
        rows.reshape(experts_n, capacity, features) for rows in (rows_fwd, rows_bwd, rows_grad)
    ]
    all_fwd, all_bwd, all_grad = [
        rows.reshape(-1, features) for rows in outward_call(packed, experts_n)
    ]
    results = (
        expert_forward(all_fwd, gate_cols, up_cols, down_rows),
        expert_backward(all_bwd, all_grad, gate_cols, up_cols, down_rows),
    )
    partial = [
        result.astype(jnp.bfloat16).reshape(experts_n, SHARDS, capacity, features)
        for result in results
    ]
    back_fwd, back_bwd = [rows.reshape(-1, features) for rows in return_call(partial)]
    mixture = gates_fwd[0] * pick(select_fwd.T, back_fwd)
    layer_out = (entering.astype(jnp.float32) + mixture).astype(jnp.bfloat16)
    grad_normed = pick(select_bwd.T, back_bwd)

    def norm_only(values):
        return normed(values, gain_row)

    unused, pullback = jax.vjp(norm_only, stashed.astype(jnp.float32))
    grad_input = (upstream.astype(jnp.float32) + pullback(grad_normed)[0]).astype(jnp.bfloat16)
    fwd_next = from_behind(layer_out[None], "section", 1)
    grad_next = from_behind(grad_input[None], "section", -1)
    return (fwd_next, grad_next)


def solution(mesh):
    return jax.shard_map(
        local,
        mesh=mesh,
        in_specs=(
            P("section", "expert", None),
            P("section", "expert", None),
            P("section", "expert", None),
            P("section", "expert", None),
            P("section", "expert", None),
            P("section", "expert", None),
            P("section", "expert", None),
            P("section", None),
            P("section", None, "expert"),
            P("section", None, "expert"),
            P("section", "expert", None),
        ),
        out_specs=(P("section", "expert", None), P("section", "expert", None)),
        check_vma=False,
    )
```

```python
import functools

import jax
import jax.numpy as jnp
from jax import lax
from jax.experimental import pallas as pl
from jax.experimental.pallas import tpu as pltpu
from jax.sharding import PartitionSpec as P

SHARDS = 4
TOP = 1


EPS = 1e-06


def normed(token_rows, gain_row):
    values = token_rows.astype(jnp.float32)
    factor = lax.rsqrt(jnp.mean(values * values, axis=-1, keepdims=True) + EPS)
    return values * factor * gain_row


def slot_tables(route_ids, gate_vals, experts_n, capacity):
    tok_rows, top_n = route_ids.shape
    flat_ids = route_ids.reshape(-1)
    one_hot = (flat_ids[:, None] == jnp.arange(experts_n, dtype=jnp.int32)[None, :]).astype(
        jnp.int32
    )
    slot_ids = jnp.sum((jnp.cumsum(one_hot, axis=0) - one_hot) * one_hot, axis=1)
    position = flat_ids * capacity + slot_ids
    places = jnp.arange(experts_n * capacity, dtype=jnp.int32)
    hit = position[None, :] == places[:, None]
    slot_gate = jnp.sum(jnp.where(hit, gate_vals.reshape(-1)[None, :], jnp.float32(0.0)), axis=1)
    select = jnp.sum(hit.reshape(-1, tok_rows, top_n), axis=2).astype(jnp.bfloat16)
    return select, slot_gate


def pick(select, rows):
    return jnp.dot(select, rows, preferred_element_type=jnp.float32)


def expert_forward(token_rows, gate_cols, up_cols, down_rows):
    pre_gate = jnp.dot(token_rows, gate_cols, preferred_element_type=jnp.float32)
    pre_up = jnp.dot(token_rows, up_cols, preferred_element_type=jnp.float32)
    hidden = (pre_gate * jax.nn.sigmoid(pre_gate) * pre_up).astype(jnp.bfloat16)
    return jnp.dot(hidden, down_rows, preferred_element_type=jnp.float32)


def expert_backward(token_rows, upstream, gate_cols, up_cols, down_rows):
    pre_gate = jnp.dot(token_rows, gate_cols, preferred_element_type=jnp.float32)
    pre_up = jnp.dot(token_rows, up_cols, preferred_element_type=jnp.float32)
    contract = (((1,), (1,)), ((), ()))
    grad_hidden = lax.dot_general(upstream, down_rows, contract, preferred_element_type=jnp.float32)
    sigmoid_gate = jax.nn.sigmoid(pre_gate)
    grad_gate = (
        grad_hidden * pre_up * sigmoid_gate * (1.0 + pre_gate * (1.0 - sigmoid_gate))
    ).astype(jnp.bfloat16)
    grad_up = (grad_hidden * pre_gate * sigmoid_gate).astype(jnp.bfloat16)
    first = lax.dot_general(grad_gate, gate_cols, contract, preferred_element_type=jnp.float32)
    second = lax.dot_general(grad_up, up_cols, contract, preferred_element_type=jnp.float32)
    return first + second


MESH = pl.DeviceIdType.MESH
VMEM_BYTES = 58 * 1024 * 1024


def places(experts_n):
    me = lax.axis_index("expert")
    group, shard = me // SHARDS, me % SHARDS
    near = shard + 1 - 2 * (shard % 2)
    mirrored, shifted = SHARDS - 1 - shard, (shard + 2) % SHARDS
    if experts_n == 2:
        return group, shard, (near, shifted), mirrored
    return group, shard, (near, mirrored), shifted


def pieces(features, experts_n):
    first = features // 4 * 3 if experts_n == 2 else features // 2
    return pl.ds(0, first), pl.ds(first, features - first)


def section_at(by):
    sections = lax.axis_size("section")
    return (lax.axis_index("section") + by + sections) % sections


def greet(partners):
    barrier = pltpu.get_barrier_semaphore()
    for section, expert in partners:
        pl.semaphore_signal(
            barrier, inc=1, device_id={"section": section, "expert": expert}, device_id_type=MESH
        )
    pl.semaphore_wait(barrier, len(partners))


def remote(src, dst, send, recv, target, by=0):
    return pltpu.make_async_remote_copy(
        src_ref=src,
        dst_ref=dst,
        send_sem=send,
        recv_sem=recv,
        device_id={"section": section_at(by), "expert": target},
        device_id_type=MESH,
    )


def outward_kernel(experts_n, arrays, shifts, *refs):
    extras = len(shifts)
    inputs, outputs = refs[: arrays + extras], refs[arrays + extras : 2 * (arrays + extras)]
    packed, passed = inputs[:arrays], inputs[arrays:]
    gathered, arrived = outputs[:arrays], outputs[arrays:]
    (
        cross_send,
        cross_recv,
        ring_send,
        ring_recv,
        part_send,
        part_recv,
        local_sem,
        pass_send,
        pass_recv,
    ) = refs[2 * (arrays + extras) :]
    group, shard, links, far = places(experts_n)
    me = lax.axis_index("expert")
    here = section_at(0)
    greet(
        [(here, group * SHARDS + link) for link in links]
        + [(here, (group + step) % experts_n * SHARDS + shard) for step in range(1, experts_n)]
        + [(section_at(by), me) for by in (1, -1)]
    )
    cols = pieces(packed[0].shape[2], experts_n)
    started = []

    def begin(copy):
        copy.start()
        started.append(copy)
        return copy

    crossing, ring, parts, local = {}, {}, {}, []
    for a in range(arrays):
        for step in range(1, experts_n):
            expert = (group + step) % experts_n
            crossing[a, step] = begin(
                remote(
                    packed[a].at[expert],
                    gathered[a].at[group, shard],
                    cross_send.at[a, step],
                    cross_recv.at[a, step],
                    expert * SHARDS + shard,
                )
            )
        for side, target in enumerate(links):
            ring[a, 0, side] = begin(
                remote(
                    packed[a].at[group],
                    gathered[a].at[group, shard],
                    ring_send.at[a, 0, side],
                    ring_recv.at[a, 0, side],
                    group * SHARDS + target,
                )
            )
        copy = pltpu.make_async_copy(
            packed[a].at[group], gathered[a].at[group, shard], local_sem.at[a]
        )
        copy.start()
        local.append(copy)
    passing = [
        begin(remote(passed[i], arrived[i], pass_send.at[i], pass_recv.at[i], me, by))
        for i, by in enumerate(shifts)
    ]

    def relay(a, step):
        origin = (group + experts_n - step) % experts_n
        for side, target in enumerate(links):
            ring[a, step, 1 - side].wait_recv()
            block = gathered[a].at[origin, links[1 - side], :, cols[side]]
            parts[a, step, side] = begin(
                remote(
                    block,
                    block,
                    part_send.at[a, step, side],
                    part_recv.at[a, step, side],
                    group * SHARDS + target,
                )
            )

    for a in range(arrays):
        for step in range(1, experts_n):
            origin = (group + experts_n - step) % experts_n
            crossing[a, step].wait_recv()
            block = gathered[a].at[origin, shard]
            for side, target in enumerate(links):
                ring[a, step, side] = begin(
                    remote(
                        block,
                        block,
                        ring_send.at[a, step, side],
                        ring_recv.at[a, step, side],
                        group * SHARDS + target,
                    )
                )
        relay(a, 0)
        if a > 0:
            for step in range(1, experts_n):
                relay(a - 1, step)
    for step in range(1, experts_n):
        relay(arrays - 1, step)
    for copy in list(parts.values()) + passing:
        copy.wait_recv()
    for copy in local:
        copy.wait()
    for copy in started:
        copy.wait_send()


def outward_call(packed, passed, shifts):
    arrays, extras = len(packed), len(passed)
    experts_n, capacity, features = packed[0].shape
    dma = pltpu.SemaphoreType.DMA
    shape = jax.ShapeDtypeStruct((experts_n, SHARDS, capacity, features), jnp.bfloat16)
    outs = pl.pallas_call(
        functools.partial(outward_kernel, experts_n, arrays, shifts),
        out_shape=[shape] * arrays + [jax.ShapeDtypeStruct(v.shape, v.dtype) for v in passed],
        in_specs=[pl.BlockSpec(memory_space=pl.ANY)] * (arrays + extras),
        out_specs=[pl.BlockSpec(memory_space=pl.ANY)] * (arrays + extras),
        scratch_shapes=[
            dma((arrays, experts_n)),
            dma((arrays, experts_n)),
            dma((arrays, experts_n, 2)),
            dma((arrays, experts_n, 2)),
            dma((arrays, experts_n, 2)),
            dma((arrays, experts_n, 2)),
            dma((arrays,)),
            dma((extras,)),
            dma((extras,)),
        ],
        compiler_params=pltpu.CompilerParams(
            collective_id=0, has_side_effects=True, vmem_limit_bytes=VMEM_BYTES
        ),
        name="rows_to_experts",
    )(*packed, *passed)
    return outs[:arrays], outs[arrays:]


def add_into(dst, terms, columns):
    tile = 512 if columns % 512 == 0 else 256 if columns % 256 == 0 else 128

    @pl.loop(0, columns // tile)
    def _(i):
        at = pl.ds(pl.multiple_of(i * tile, tile), tile)
        total = terms[0][:, at].astype(jnp.float32)
        for term in terms[1:]:
            total = total + term[:, at].astype(jnp.float32)
        dst[:, at] = total.astype(dst.dtype)


def return_kernel(experts_n, shifts, *refs):
    arrays = len(shifts)
    partial, summed = refs[:arrays], refs[arrays : 2 * arrays]
    (
        far_first,
        far_second,
        near_in,
        total,
        far_send,
        far_recv,
        near_send,
        near_recv,
        out_send,
        out_recv,
    ) = refs[2 * arrays :]
    far_in = (far_first, far_second)
    group, shard, links, far = places(experts_n)
    here = section_at(0)
    greet(
        [(here, group * SHARDS + link) for link in links]
        + [
            (section_at(by), expert * SHARDS + shard)
            for by in (1, -1)
            for expert in range(experts_n)
        ]
    )
    features = partial[0].shape[3]
    cols = pieces(features, experts_n)
    started, far_copies, near_copies, out_copies = [], {}, {}, {}

    def begin(copy):
        copy.start()
        started.append(copy)
        return copy

    order = [(a, step) for a in range(arrays) for step in list(range(1, experts_n)) + [0]]
    for a, step in order:
        origin = (group + step) % experts_n
        for side, target in enumerate(links):
            far_copies[a, step, side] = begin(
                remote(
                    partial[a].at[origin, far, :, cols[side]],
                    far_in[side].at[a, step],
                    far_send.at[a, step, side],
                    far_recv.at[a, step, side],
                    group * SHARDS + target,
                )
            )
    for a, step in order:
        origin = (group + step) % experts_n
        for side, target in enumerate(links):
            near_copies[a, step, side, 1] = begin(
                remote(
                    partial[a].at[origin, target, :, cols[side]],
                    near_in.at[a, step, side, :, cols[side]],
                    near_send.at[a, step, side, 1],
                    near_recv.at[a, step, side, 1],
                    group * SHARDS + target,
                )
            )
    for a, step in order:
        origin = (group + step) % experts_n
        for side in range(2):
            target = links[1 - side]
            far_copies[a, step, side].wait_recv()
            block = far_in[side].at[a, step]
            add_into(block, (block, partial[a].at[origin, target, :, cols[side]]), cols[side].size)
            near_copies[a, step, 1 - side, 0] = begin(
                remote(
                    block,
                    near_in.at[a, step, 1 - side, :, cols[side]],
                    near_send.at[a, step, 1 - side, 0],
                    near_recv.at[a, step, 1 - side, 0],
                    group * SHARDS + target,
                )
            )
    for a, step in order:
        origin = (group + step) % experts_n
        for side in range(2):
            for part in range(2):
                near_copies[a, step, side, part].wait_recv()
        result = total.at[a, step]
        add_into(
            result,
            (near_in.at[a, step, 0], near_in.at[a, step, 1], partial[a].at[origin, shard]),
            features,
        )
        out_copies[a, step] = begin(
            remote(
                result,
                summed[a].at[group],
                out_send.at[a, step],
                out_recv.at[a, step],
                origin * SHARDS + shard,
                shifts[a],
            )
        )
    for copy in out_copies.values():
        copy.wait_recv()
    for copy in started:
        copy.wait_send()


def return_call(partial, shifts):
    arrays = len(partial)
    experts_n, unused, capacity, features = partial[0].shape
    dma = pltpu.SemaphoreType.DMA
    shape = jax.ShapeDtypeStruct((experts_n, capacity, features), jnp.bfloat16)
    first, second = pieces(features, experts_n)
    return pl.pallas_call(
        functools.partial(return_kernel, experts_n, shifts),
        out_shape=[shape] * arrays,
        in_specs=[pl.BlockSpec(memory_space=pltpu.VMEM)] * arrays,
        out_specs=[pl.BlockSpec(memory_space=pl.ANY)] * arrays,
        scratch_shapes=[
            pltpu.VMEM((arrays, experts_n, capacity, first.size), jnp.bfloat16),
            pltpu.VMEM((arrays, experts_n, capacity, second.size), jnp.bfloat16),
            pltpu.VMEM((arrays, experts_n, 2, capacity, features), jnp.bfloat16),
            pltpu.VMEM((arrays, experts_n, capacity, features), jnp.bfloat16),
            dma((arrays, experts_n, 2)),
            dma((arrays, experts_n, 2)),
            dma((arrays, experts_n, 2, 2)),
            dma((arrays, experts_n, 2, 2)),
            dma((arrays, experts_n)),
            dma((arrays, experts_n)),
        ],
        compiler_params=pltpu.CompilerParams(
            collective_id=1, has_side_effects=True, vmem_limit_bytes=VMEM_BYTES
        ),
        name="sums_to_tokens",
    )(*partial)


def local(
    acts_fwd,
    routes_fwd,
    gates_fwd,
    stash_bwd,
    grads_bwd,
    routes_bwd,
    gates_bwd,
    gain,
    w_gate,
    w_up,
    w_down,
):
    devices = lax.axis_size("expert")
    experts_n = devices // SHARDS
    tok_rows, features = acts_fwd.shape[1:]
    capacity = min(tok_rows, 9 * tok_rows * TOP // (8 * experts_n))
    gate_cols = w_gate[0]
    up_cols = w_up[0]
    down_rows = w_down[0]
    gain_row = gain[0]
    entering = acts_fwd[0]
    select_fwd, unused_gate = slot_tables(routes_fwd[0], gates_fwd[0], experts_n, capacity)
    rows_fwd = pick(select_fwd, normed(entering, gain_row).astype(jnp.bfloat16)).astype(jnp.bfloat16)
    stashed = stash_bwd[0]
    upstream = grads_bwd[0]
    select_bwd, slot_gate = slot_tables(routes_bwd[0], gates_bwd[0], experts_n, capacity)
    rows_bwd = pick(select_bwd, normed(stashed, gain_row).astype(jnp.bfloat16)).astype(jnp.bfloat16)
    rows_grad = (pick(select_bwd, upstream) * slot_gate[:, None]).astype(jnp.bfloat16)
    packed = [
        rows.reshape(experts_n, capacity, features) for rows in (rows_fwd, rows_bwd, rows_grad)
    ]
    wide = -(-experts_n * capacity // 128) * 128

    def token_table(select):
        return jnp.pad(select.T, ((0, 0), (0, wide - experts_n * capacity)))

    passed = (
        (acts_fwd, 1),
        (token_table(select_fwd), 1),
        (jnp.broadcast_to(gates_fwd[0], (tok_rows, 128)), 1),
        (stash_bwd, -1),
        (grads_bwd, -1),
        (token_table(select_bwd), -1),
        (gain.reshape(features // 128, 128), -1),
    )
    gathered, arrived = outward_call(
        packed, [value for value, by in passed], tuple(by for value, by in passed)
    )
    all_fwd, all_bwd, all_grad = [rows.reshape(-1, features) for rows in gathered]
    results = (
        expert_forward(all_fwd, gate_cols, up_cols, down_rows),
        expert_backward(all_bwd, all_grad, gate_cols, up_cols, down_rows),
    )
    partial = [
        result.astype(jnp.bfloat16).reshape(experts_n, SHARDS, capacity, features)
        for result in results
    ]
    back_fwd, back_bwd = [rows.reshape(-1, features) for rows in return_call(partial, (1, -1))]
    acts, table_fwd, gates, stash, grads, table_bwd, gain_there = arrived
    filled = experts_n * capacity
    mixture = gates[:, :1] * pick(table_fwd[:, :filled], back_fwd)
    layer_out = (acts[0].astype(jnp.float32) + mixture).astype(jnp.bfloat16)
    grad_normed = pick(table_bwd[:, :filled], back_bwd)
    gain_row = gain_there.reshape(features)

    def norm_only(values):
        return normed(values, gain_row)

    unused, pullback = jax.vjp(norm_only, stash[0].astype(jnp.float32))
    grad_input = (grads[0].astype(jnp.float32) + pullback(grad_normed)[0]).astype(jnp.bfloat16)
    return (layer_out[None], grad_input[None])


def solution(mesh):
    return jax.shard_map(
        local,
        mesh=mesh,
        in_specs=(
            P("section", "expert", None),
            P("section", "expert", None),
            P("section", "expert", None),
            P("section", "expert", None),
            P("section", "expert", None),
            P("section", "expert", None),
            P("section", "expert", None),
            P("section", None),
            P("section", None, "expert"),
            P("section", None, "expert"),
            P("section", "expert", None),
        ),
        out_specs=(P("section", "expert", None), P("section", "expert", None)),
        check_vma=False,
    )
```

```python
import functools

import jax
import jax.numpy as jnp
from jax import lax
from jax.experimental import pallas as pl
from jax.experimental.pallas import tpu as pltpu
from jax.sharding import PartitionSpec as P

SHARDS = 4
TOP = 1


EPS = 1e-06


def normed(token_rows, gain_row):
    values = token_rows.astype(jnp.float32)
    factor = lax.rsqrt(jnp.mean(values * values, axis=-1, keepdims=True) + EPS)
    return values * factor * gain_row


def slot_tables(route_ids, gate_vals, experts_n, capacity):
    tok_rows, top_n = route_ids.shape
    flat_ids = route_ids.reshape(-1)
    one_hot = (flat_ids[:, None] == jnp.arange(experts_n, dtype=jnp.int32)[None, :]).astype(
        jnp.int32
    )
    slot_ids = jnp.sum((jnp.cumsum(one_hot, axis=0) - one_hot) * one_hot, axis=1)
    position = flat_ids * capacity + slot_ids
    places = jnp.arange(experts_n * capacity, dtype=jnp.int32)
    hit = position[None, :] == places[:, None]
    slot_gate = jnp.sum(jnp.where(hit, gate_vals.reshape(-1)[None, :], jnp.float32(0.0)), axis=1)
    select = jnp.sum(hit.reshape(-1, tok_rows, top_n), axis=2).astype(jnp.bfloat16)
    return select, slot_gate


def pick(select, rows):
    return jnp.dot(select, rows, preferred_element_type=jnp.float32)


def expert_forward(token_rows, gate_cols, up_cols, down_rows):
    pre_gate = jnp.dot(token_rows, gate_cols, preferred_element_type=jnp.float32)
    pre_up = jnp.dot(token_rows, up_cols, preferred_element_type=jnp.float32)
    hidden = (pre_gate * jax.nn.sigmoid(pre_gate) * pre_up).astype(jnp.bfloat16)
    return jnp.dot(hidden, down_rows, preferred_element_type=jnp.float32)


def expert_backward(token_rows, upstream, gate_cols, up_cols, down_rows):
    pre_gate = jnp.dot(token_rows, gate_cols, preferred_element_type=jnp.float32)
    pre_up = jnp.dot(token_rows, up_cols, preferred_element_type=jnp.float32)
    contract = (((1,), (1,)), ((), ()))
    grad_hidden = lax.dot_general(upstream, down_rows, contract, preferred_element_type=jnp.float32)
    sigmoid_gate = jax.nn.sigmoid(pre_gate)
    grad_gate = (
        grad_hidden * pre_up * sigmoid_gate * (1.0 + pre_gate * (1.0 - sigmoid_gate))
    ).astype(jnp.bfloat16)
    grad_up = (grad_hidden * pre_gate * sigmoid_gate).astype(jnp.bfloat16)
    first = lax.dot_general(grad_gate, gate_cols, contract, preferred_element_type=jnp.float32)
    second = lax.dot_general(grad_up, up_cols, contract, preferred_element_type=jnp.float32)
    return first + second


MESH = pl.DeviceIdType.MESH
VMEM_BYTES = 58 * 1024 * 1024
CHUNKS = 2
WINDOW = 2


def places(experts_n):
    me = lax.axis_index("expert")
    group, shard = me // SHARDS, me % SHARDS
    near = shard + 1 - 2 * (shard % 2)
    mirrored, shifted = SHARDS - 1 - shard, (shard + 2) % SHARDS
    if experts_n == 2:
        return group, shard, (near, shifted), mirrored
    return group, shard, (near, mirrored), shifted


def pieces(features, experts_n, start=0):
    first = features // 4 * 3 if experts_n == 2 else features // 2
    return pl.ds(start, first), pl.ds(start + first, features - first)


def section_at(by):
    sections = lax.axis_size("section")
    return (lax.axis_index("section") + by + sections) % sections


def greet(partners):
    barrier = pltpu.get_barrier_semaphore()
    for section, expert in partners:
        pl.semaphore_signal(
            barrier, inc=1, device_id={"section": section, "expert": expert}, device_id_type=MESH
        )
    pl.semaphore_wait(barrier, len(partners))


def remote(src, dst, send, recv, target, by=0):
    return pltpu.make_async_remote_copy(
        src_ref=src,
        dst_ref=dst,
        send_sem=send,
        recv_sem=recv,
        device_id={"section": section_at(by), "expert": target},
        device_id_type=MESH,
    )


def outward_kernel(experts_n, arrays, shifts, *refs):
    extras = len(shifts)
    inputs, outputs = refs[: arrays + extras], refs[arrays + extras : 2 * (arrays + extras)]
    packed, passed = inputs[:arrays], inputs[arrays:]
    gathered, arrived = outputs[:arrays], outputs[arrays:]
    (
        cross_send,
        cross_recv,
        ring_send,
        ring_recv,
        part_send,
        part_recv,
        local_sem,
        pass_send,
        pass_recv,
    ) = refs[2 * (arrays + extras) :]
    group, shard, links, far = places(experts_n)
    me = lax.axis_index("expert")
    here = section_at(0)
    greet(
        [(here, group * SHARDS + link) for link in links]
        + [(here, (group + step) % experts_n * SHARDS + shard) for step in range(1, experts_n)]
        + [(section_at(by), me) for by in (1, -1)]
    )
    cols = pieces(packed[0].shape[2], experts_n)
    started = []

    def begin(copy):
        copy.start()
        started.append(copy)
        return copy

    crossing, ring, parts, local = {}, {}, {}, []
    for a in range(arrays):
        for step in range(1, experts_n):
            expert = (group + step) % experts_n
            crossing[a, step] = begin(
                remote(
                    packed[a].at[expert],
                    gathered[a].at[group, shard],
                    cross_send.at[a, step],
                    cross_recv.at[a, step],
                    expert * SHARDS + shard,
                )
            )
        for side, target in enumerate(links):
            ring[a, 0, side] = begin(
                remote(
                    packed[a].at[group],
                    gathered[a].at[group, shard],
                    ring_send.at[a, 0, side],
                    ring_recv.at[a, 0, side],
                    group * SHARDS + target,
                )
            )
        copy = pltpu.make_async_copy(
            packed[a].at[group], gathered[a].at[group, shard], local_sem.at[a]
        )
        copy.start()
        local.append(copy)
    passing = [
        begin(remote(passed[i], arrived[i], pass_send.at[i], pass_recv.at[i], me, by))
        for i, by in enumerate(shifts)
    ]

    def relay(a, step):
        origin = (group + experts_n - step) % experts_n
        for side, target in enumerate(links):
            ring[a, step, 1 - side].wait_recv()
            block = gathered[a].at[origin, links[1 - side], :, cols[side]]
            parts[a, step, side] = begin(
                remote(
                    block,
                    block,
                    part_send.at[a, step, side],
                    part_recv.at[a, step, side],
                    group * SHARDS + target,
                )
            )

    for a in range(arrays):
        for step in range(1, experts_n):
            origin = (group + experts_n - step) % experts_n
            crossing[a, step].wait_recv()
            block = gathered[a].at[origin, shard]
            for side, target in enumerate(links):
                ring[a, step, side] = begin(
                    remote(
                        block,
                        block,
                        ring_send.at[a, step, side],
                        ring_recv.at[a, step, side],
                        group * SHARDS + target,
                    )
                )
        relay(a, 0)
        if a > 0:
            for step in range(1, experts_n):
                relay(a - 1, step)
    for step in range(1, experts_n):
        relay(arrays - 1, step)
    for copy in list(parts.values()) + passing:
        copy.wait_recv()
    for copy in local:
        copy.wait()
    for copy in started:
        copy.wait_send()


def outward_call(packed, passed, shifts):
    arrays, extras = len(packed), len(passed)
    experts_n, capacity, features = packed[0].shape
    dma = pltpu.SemaphoreType.DMA
    shape = jax.ShapeDtypeStruct((experts_n, SHARDS, capacity, features), jnp.bfloat16)
    outs = pl.pallas_call(
        functools.partial(outward_kernel, experts_n, arrays, shifts),
        out_shape=[shape] * arrays + [jax.ShapeDtypeStruct(v.shape, v.dtype) for v in passed],
        in_specs=[pl.BlockSpec(memory_space=pl.ANY)] * (arrays + extras),
        out_specs=[pl.BlockSpec(memory_space=pl.ANY)] * (arrays + extras),
        scratch_shapes=[
            dma((arrays, experts_n)),
            dma((arrays, experts_n)),
            dma((arrays, experts_n, 2)),
            dma((arrays, experts_n, 2)),
            dma((arrays, experts_n, 2)),
            dma((arrays, experts_n, 2)),
            dma((arrays,)),
            dma((extras,)),
            dma((extras,)),
        ],
        compiler_params=pltpu.CompilerParams(
            collective_id=0, has_side_effects=True, vmem_limit_bytes=VMEM_BYTES
        ),
        name="rows_to_experts",
    )(*packed, *passed)
    return outs[:arrays], outs[arrays:]


def add_into(dst, terms, columns):
    tile = 512 if columns % 512 == 0 else 256 if columns % 256 == 0 else 128

    @pl.loop(0, columns // tile)
    def _(i):
        at = pl.ds(pl.multiple_of(i * tile, tile), tile)
        total = terms[0][:, at].astype(jnp.float32)
        for term in terms[1:]:
            total = total + term[:, at].astype(jnp.float32)
        dst[:, at] = total.astype(dst.dtype)


def return_kernel(experts_n, shifts, *refs):
    arrays = len(shifts)
    partial, summed = refs[:arrays], refs[arrays : 2 * arrays]
    (
        far_first,
        far_second,
        near_in,
        total,
        far_send,
        far_recv,
        near_send,
        near_recv,
        out_send,
        out_recv,
    ) = refs[2 * arrays :]
    far_in = (far_first, far_second)
    group, shard, links, far = places(experts_n)
    here = section_at(0)
    greet(
        [(here, group * SHARDS + link) for link in links]
        + [
            (section_at(by), expert * SHARDS + shard)
            for by in (1, -1)
            for expert in range(experts_n)
        ]
    )
    width = partial[0].shape[3] // CHUNKS
    started, far_copies, near_copies, out_copies = [], {}, {}, {}

    def begin(copy):
        copy.start()
        started.append(copy)
        return copy

    order = [
        (a, step, c)
        for step in list(range(1, experts_n)) + [0]
        for a in range(arrays)
        for c in range(CHUNKS)
    ]

    def columns(c):
        return pieces(width, experts_n, c * width)

    def send(a, step, c):
        origin = (group + step) % experts_n
        cols = columns(c)
        for side, target in enumerate(links):
            far_copies[a, step, c, side] = begin(
                remote(
                    partial[a].at[origin, far, :, cols[side]],
                    far_in[side].at[a, step, c],
                    far_send.at[a, step, c, side],
                    far_recv.at[a, step, c, side],
                    group * SHARDS + target,
                )
            )
        for side, target in enumerate(links):
            near_copies[a, step, c, side, 1] = begin(
                remote(
                    partial[a].at[origin, target, :, cols[side]],
                    near_in.at[a, step, side, :, cols[side]],
                    near_send.at[a, step, c, side, 1],
                    near_recv.at[a, step, c, side, 1],
                    group * SHARDS + target,
                )
            )

    def merge(a, step, c):
        origin = (group + step) % experts_n
        cols = columns(c)
        for side in range(2):
            target = links[1 - side]
            far_copies[a, step, c, side].wait_recv()
            block = far_in[side].at[a, step, c]
            add_into(block, (block, partial[a].at[origin, target, :, cols[side]]), cols[side].size)
            near_copies[a, step, c, 1 - side, 0] = begin(
                remote(
                    block,
                    near_in.at[a, step, 1 - side, :, cols[side]],
                    near_send.at[a, step, c, 1 - side, 0],
                    near_recv.at[a, step, c, 1 - side, 0],
                    group * SHARDS + target,
                )
            )

    def finish(a, step, c):
        origin = (group + step) % experts_n
        whole = pl.ds(c * width, width)
        for side in range(2):
            for part in range(2):
                near_copies[a, step, c, side, part].wait_recv()
        result = total.at[a, step, :, whole]
        add_into(
            result,
            (
                near_in.at[a, step, 0, :, whole],
                near_in.at[a, step, 1, :, whole],
                partial[a].at[origin, shard, :, whole],
            ),
            width,
        )
        out_copies[a, step, c] = begin(
            remote(
                result,
                summed[a].at[group, :, whole],
                out_send.at[a, step, c],
                out_recv.at[a, step, c],
                origin * SHARDS + shard,
                shifts[a],
            )
        )

    for item in order[:WINDOW]:
        send(*item)
    for i, item in enumerate(order):
        merge(*item)
        if i + WINDOW < len(order):
            send(*order[i + WINDOW])
        if i > 0:
            finish(*order[i - 1])
    finish(*order[-1])
    for copy in out_copies.values():
        copy.wait_recv()
    for copy in started:
        copy.wait_send()


def return_call(partial, shifts):
    arrays = len(partial)
    experts_n, unused, capacity, features = partial[0].shape
    dma = pltpu.SemaphoreType.DMA
    shape = jax.ShapeDtypeStruct((experts_n, capacity, features), jnp.bfloat16)
    first, second = pieces(features // CHUNKS, experts_n)
    return pl.pallas_call(
        functools.partial(return_kernel, experts_n, shifts),
        out_shape=[shape] * arrays,
        in_specs=[pl.BlockSpec(memory_space=pltpu.VMEM)] * arrays,
        out_specs=[pl.BlockSpec(memory_space=pl.ANY)] * arrays,
        scratch_shapes=[
            pltpu.VMEM((arrays, experts_n, CHUNKS, capacity, first.size), jnp.bfloat16),
            pltpu.VMEM((arrays, experts_n, CHUNKS, capacity, second.size), jnp.bfloat16),
            pltpu.VMEM((arrays, experts_n, 2, capacity, features), jnp.bfloat16),
            pltpu.VMEM((arrays, experts_n, capacity, features), jnp.bfloat16),
            dma((arrays, experts_n, CHUNKS, 2)),
            dma((arrays, experts_n, CHUNKS, 2)),
            dma((arrays, experts_n, CHUNKS, 2, 2)),
            dma((arrays, experts_n, CHUNKS, 2, 2)),
            dma((arrays, experts_n, CHUNKS)),
            dma((arrays, experts_n, CHUNKS)),
        ],
        compiler_params=pltpu.CompilerParams(
            collective_id=1, has_side_effects=True, vmem_limit_bytes=VMEM_BYTES
        ),
        name="sums_to_tokens",
    )(*partial)


def local(
    acts_fwd,
    routes_fwd,
    gates_fwd,
    stash_bwd,
    grads_bwd,
    routes_bwd,
    gates_bwd,
    gain,
    w_gate,
    w_up,
    w_down,
):
    devices = lax.axis_size("expert")
    experts_n = devices // SHARDS
    tok_rows, features = acts_fwd.shape[1:]
    capacity = min(tok_rows, 9 * tok_rows * TOP // (8 * experts_n))
    gate_cols = w_gate[0]
    up_cols = w_up[0]
    down_rows = w_down[0]
    gain_row = gain[0]
    entering = acts_fwd[0]
    select_fwd, unused_gate = slot_tables(routes_fwd[0], gates_fwd[0], experts_n, capacity)
    rows_fwd = pick(select_fwd, normed(entering, gain_row).astype(jnp.bfloat16)).astype(jnp.bfloat16)
    stashed = stash_bwd[0]
    upstream = grads_bwd[0]
    select_bwd, slot_gate = slot_tables(routes_bwd[0], gates_bwd[0], experts_n, capacity)
    rows_bwd = pick(select_bwd, normed(stashed, gain_row).astype(jnp.bfloat16)).astype(jnp.bfloat16)
    rows_grad = (pick(select_bwd, upstream) * slot_gate[:, None]).astype(jnp.bfloat16)
    packed = [
        rows.reshape(experts_n, capacity, features) for rows in (rows_fwd, rows_bwd, rows_grad)
    ]
    wide = -(-experts_n * capacity // 128) * 128

    def token_table(select):
        return jnp.pad(select.T, ((0, 0), (0, wide - experts_n * capacity)))

    passed = (
        (acts_fwd, 1),
        (token_table(select_fwd), 1),
        (jnp.broadcast_to(gates_fwd[0], (tok_rows, 128)), 1),
        (stash_bwd, -1),
        (grads_bwd, -1),
        (token_table(select_bwd), -1),
        (gain.reshape(features // 128, 128), -1),
    )
    gathered, arrived = outward_call(
        packed, [value for value, by in passed], tuple(by for value, by in passed)
    )
    all_fwd, all_bwd, all_grad = [rows.reshape(-1, features) for rows in gathered]
    results = (
        expert_forward(all_fwd, gate_cols, up_cols, down_rows),
        expert_backward(all_bwd, all_grad, gate_cols, up_cols, down_rows),
    )
    partial = [
        result.astype(jnp.bfloat16).reshape(experts_n, SHARDS, capacity, features)
        for result in results
    ]
    back_fwd, back_bwd = [rows.reshape(-1, features) for rows in return_call(partial, (1, -1))]
    acts, table_fwd, gates, stash, grads, table_bwd, gain_there = arrived
    filled = experts_n * capacity
    mixture = gates[:, :1] * pick(table_fwd[:, :filled], back_fwd)
    layer_out = (acts[0].astype(jnp.float32) + mixture).astype(jnp.bfloat16)
    grad_normed = pick(table_bwd[:, :filled], back_bwd)
    gain_row = gain_there.reshape(features)

    def norm_only(values):
        return normed(values, gain_row)

    unused, pullback = jax.vjp(norm_only, stash[0].astype(jnp.float32))
    grad_input = (grads[0].astype(jnp.float32) + pullback(grad_normed)[0]).astype(jnp.bfloat16)
    return (layer_out[None], grad_input[None])


def solution(mesh):
    return jax.shard_map(
        local,
        mesh=mesh,
        in_specs=(
            P("section", "expert", None),
            P("section", "expert", None),
            P("section", "expert", None),
            P("section", "expert", None),
            P("section", "expert", None),
            P("section", "expert", None),
            P("section", "expert", None),
            P("section", None),
            P("section", None, "expert"),
            P("section", None, "expert"),
            P("section", "expert", None),
        ),
        out_specs=(P("section", "expert", None), P("section", "expert", None)),
        check_vma=False,
    )
```

```python
import functools

import jax
import jax.numpy as jnp
from jax import lax
from jax.experimental import pallas as pl
from jax.experimental.pallas import tpu as pltpu
from jax.sharding import PartitionSpec as P

SHARDS = 4
TOP = 1


EPS = 1e-06


def normed(token_rows, gain_row):
    values = token_rows.astype(jnp.float32)
    factor = lax.rsqrt(jnp.mean(values * values, axis=-1, keepdims=True) + EPS)
    return values * factor * gain_row


def slot_tables(route_ids, gate_vals, experts_n, capacity):
    tok_rows, top_n = route_ids.shape
    flat_ids = route_ids.reshape(-1)
    one_hot = (flat_ids[:, None] == jnp.arange(experts_n, dtype=jnp.int32)[None, :]).astype(
        jnp.int32
    )
    slot_ids = jnp.sum((jnp.cumsum(one_hot, axis=0) - one_hot) * one_hot, axis=1)
    position = flat_ids * capacity + slot_ids
    places = jnp.arange(experts_n * capacity, dtype=jnp.int32)
    hit = position[None, :] == places[:, None]
    slot_gate = jnp.sum(jnp.where(hit, gate_vals.reshape(-1)[None, :], jnp.float32(0.0)), axis=1)
    select = jnp.sum(hit.reshape(-1, tok_rows, top_n), axis=2).astype(jnp.bfloat16)
    return select, slot_gate


def pick(select, rows):
    return jnp.dot(select, rows, preferred_element_type=jnp.float32)


def expert_forward(token_rows, gate_cols, up_cols):
    pre_gate = jnp.dot(token_rows, gate_cols, preferred_element_type=jnp.float32)
    pre_up = jnp.dot(token_rows, up_cols, preferred_element_type=jnp.float32)
    return (pre_gate * jax.nn.sigmoid(pre_gate) * pre_up).astype(jnp.bfloat16)


def expert_backward(token_rows, upstream, gate_cols, up_cols, down_rows):
    pre_gate = jnp.dot(token_rows, gate_cols, preferred_element_type=jnp.float32)
    pre_up = jnp.dot(token_rows, up_cols, preferred_element_type=jnp.float32)
    contract = (((1,), (1,)), ((), ()))
    grad_hidden = lax.dot_general(upstream, down_rows, contract, preferred_element_type=jnp.float32)
    sigmoid_gate = jax.nn.sigmoid(pre_gate)
    grad_gate = (
        grad_hidden * pre_up * sigmoid_gate * (1.0 + pre_gate * (1.0 - sigmoid_gate))
    ).astype(jnp.bfloat16)
    grad_up = (grad_hidden * pre_gate * sigmoid_gate).astype(jnp.bfloat16)
    return grad_gate, grad_up


MESH = pl.DeviceIdType.MESH
VMEM_BYTES = 58 * 1024 * 1024
CHUNKS = 2
WINDOW = 2


def places(experts_n):
    me = lax.axis_index("expert")
    group, shard = me // SHARDS, me % SHARDS
    near = shard + 1 - 2 * (shard % 2)
    mirrored, shifted = SHARDS - 1 - shard, (shard + 2) % SHARDS
    if experts_n == 2:
        return group, shard, (near, shifted), mirrored
    return group, shard, (near, mirrored), shifted


def pieces(features, experts_n, start=0):
    first = features // 4 * 3 if experts_n == 2 else features // 2
    return pl.ds(start, first), pl.ds(start + first, features - first)


def section_at(by):
    sections = lax.axis_size("section")
    return (lax.axis_index("section") + by + sections) % sections


def greet(partners):
    barrier = pltpu.get_barrier_semaphore()
    for section, expert in partners:
        pl.semaphore_signal(
            barrier, inc=1, device_id={"section": section, "expert": expert}, device_id_type=MESH
        )
    pl.semaphore_wait(barrier, len(partners))


def remote(src, dst, send, recv, target, by=0):
    return pltpu.make_async_remote_copy(
        src_ref=src,
        dst_ref=dst,
        send_sem=send,
        recv_sem=recv,
        device_id={"section": section_at(by), "expert": target},
        device_id_type=MESH,
    )


def outward_kernel(experts_n, arrays, shifts, *refs):
    extras = len(shifts)
    inputs, outputs = refs[: arrays + extras], refs[arrays + extras : 2 * (arrays + extras)]
    packed, passed = inputs[:arrays], inputs[arrays:]
    gathered, arrived = outputs[:arrays], outputs[arrays:]
    (
        cross_send,
        cross_recv,
        ring_send,
        ring_recv,
        part_send,
        part_recv,
        local_sem,
        pass_send,
        pass_recv,
    ) = refs[2 * (arrays + extras) :]
    group, shard, links, far = places(experts_n)
    me = lax.axis_index("expert")
    here = section_at(0)
    greet(
        [(here, group * SHARDS + link) for link in links]
        + [(here, (group + step) % experts_n * SHARDS + shard) for step in range(1, experts_n)]
        + [(section_at(by), me) for by in (1, -1)]
    )
    cols = pieces(packed[0].shape[2], experts_n)
    started = []

    def begin(copy):
        copy.start()
        started.append(copy)
        return copy

    crossing, ring, parts, local = {}, {}, {}, []
    for a in range(arrays):
        for step in range(1, experts_n):
            expert = (group + step) % experts_n
            crossing[a, step] = begin(
                remote(
                    packed[a].at[expert],
                    gathered[a].at[group, shard],
                    cross_send.at[a, step],
                    cross_recv.at[a, step],
                    expert * SHARDS + shard,
                )
            )
        for side, target in enumerate(links):
            ring[a, 0, side] = begin(
                remote(
                    packed[a].at[group],
                    gathered[a].at[group, shard],
                    ring_send.at[a, 0, side],
                    ring_recv.at[a, 0, side],
                    group * SHARDS + target,
                )
            )
        copy = pltpu.make_async_copy(
            packed[a].at[group], gathered[a].at[group, shard], local_sem.at[a]
        )
        copy.start()
        local.append(copy)
    passing = [
        begin(remote(passed[i], arrived[i], pass_send.at[i], pass_recv.at[i], me, by))
        for i, by in enumerate(shifts)
    ]

    def relay(a, step):
        origin = (group + experts_n - step) % experts_n
        for side, target in enumerate(links):
            ring[a, step, 1 - side].wait_recv()
            block = gathered[a].at[origin, links[1 - side], :, cols[side]]
            parts[a, step, side] = begin(
                remote(
                    block,
                    block,
                    part_send.at[a, step, side],
                    part_recv.at[a, step, side],
                    group * SHARDS + target,
                )
            )

    for a in range(arrays):
        for step in range(1, experts_n):
            origin = (group + experts_n - step) % experts_n
            crossing[a, step].wait_recv()
            block = gathered[a].at[origin, shard]
            for side, target in enumerate(links):
                ring[a, step, side] = begin(
                    remote(
                        block,
                        block,
                        ring_send.at[a, step, side],
                        ring_recv.at[a, step, side],
                        group * SHARDS + target,
                    )
                )
        relay(a, 0)
        if a > 0:
            for step in range(1, experts_n):
                relay(a - 1, step)
    for step in range(1, experts_n):
        relay(arrays - 1, step)
    for copy in list(parts.values()) + passing:
        copy.wait_recv()
    for copy in local:
        copy.wait()
    for copy in started:
        copy.wait_send()


def outward_call(packed, passed, shifts):
    arrays, extras = len(packed), len(passed)
    experts_n, capacity, features = packed[0].shape
    dma = pltpu.SemaphoreType.DMA
    shape = jax.ShapeDtypeStruct((experts_n, SHARDS, capacity, features), jnp.bfloat16)
    outs = pl.pallas_call(
        functools.partial(outward_kernel, experts_n, arrays, shifts),
        out_shape=[shape] * arrays + [jax.ShapeDtypeStruct(v.shape, v.dtype) for v in passed],
        in_specs=[pl.BlockSpec(memory_space=pl.ANY)] * (arrays + extras),
        out_specs=[pl.BlockSpec(memory_space=pl.ANY)] * (arrays + extras),
        scratch_shapes=[
            dma((arrays, experts_n)),
            dma((arrays, experts_n)),
            dma((arrays, experts_n, 2)),
            dma((arrays, experts_n, 2)),
            dma((arrays, experts_n, 2)),
            dma((arrays, experts_n, 2)),
            dma((arrays,)),
            dma((extras,)),
            dma((extras,)),
        ],
        compiler_params=pltpu.CompilerParams(
            collective_id=0, has_side_effects=True, vmem_limit_bytes=VMEM_BYTES
        ),
        name="rows_to_experts",
    )(*packed, *passed)
    return outs[:arrays], outs[arrays:]


def add_into(dst, terms, columns):
    tile = 512 if columns % 512 == 0 else 256 if columns % 256 == 0 else 128

    @pl.loop(0, columns // tile)
    def _(i):
        at = pl.ds(pl.multiple_of(i * tile, tile), tile)
        total = terms[0][:, at].astype(jnp.float32)
        for term in terms[1:]:
            total = total + term[:, at].astype(jnp.float32)
        dst[:, at] = total.astype(dst.dtype)


def return_kernel(experts_n, shifts, *refs):
    arrays = len(shifts)
    hidden, grad_gate, grad_up, gate_cols, up_cols, down_rows = refs[:6]
    summed = refs[6 : 6 + arrays]
    (
        all_partial,
        far_first,
        far_second,
        near_in,
        total,
        far_send,
        far_recv,
        near_send,
        near_recv,
        out_send,
        out_recv,
    ) = refs[6 + arrays :]
    partial = [all_partial.at[a] for a in range(arrays)]
    far_in = (far_first, far_second)
    group, shard, links, far = places(experts_n)
    here = section_at(0)
    greet(
        [(here, group * SHARDS + link) for link in links]
        + [
            (section_at(by), expert * SHARDS + shard)
            for by in (1, -1)
            for expert in range(experts_n)
        ]
    )
    capacity, features = summed[0].shape[1:]
    width = features // CHUNKS
    contract = (((1,), (1,)), ((), ()))

    def product(a, block, at):
        rows = (hidden,) if a == 0 else (grad_gate, grad_up)
        rows = [ref[...] if block is None else ref[block] for ref in rows]
        if a == 0:
            return jnp.dot(rows[0], down_rows[:, at], preferred_element_type=jnp.float32)
        return lax.dot_general(
            rows[0], gate_cols[at, :], contract, preferred_element_type=jnp.float32
        ) + lax.dot_general(rows[1], up_cols[at, :], contract, preferred_element_type=jnp.float32)

    def compute(a, c):
        tile = 512 if width % 512 == 0 else 128

        @pl.loop(0, width // tile)
        def _(i):
            at = pl.ds(pl.multiple_of(c * width + i * tile, tile), tile)
            if len(hidden.shape) == 2:
                block = product(a, None, at).reshape(experts_n, SHARDS, capacity, tile)
                all_partial[a, :, :, :, at] = block.astype(jnp.bfloat16)
            else:
                for o in range(experts_n):
                    for d in range(SHARDS):
                        block = product(a, o * SHARDS + d, at)
                        all_partial[a, o, d, :, at] = block.astype(jnp.bfloat16)

    started, far_copies, near_copies, out_copies = [], {}, {}, {}

    def begin(copy):
        copy.start()
        started.append(copy)
        return copy

    order = [
        (a, step, c)
        for step in list(range(1, experts_n)) + [0]
        for a in range(arrays)
        for c in range(CHUNKS)
    ]

    def columns(c):
        return pieces(width, experts_n, c * width)

    computed = set()

    def send(a, step, c):
        if (a, c) not in computed:
            computed.add((a, c))
            compute(a, c)
        origin = (group + step) % experts_n
        cols = columns(c)
        for side, target in enumerate(links):
            far_copies[a, step, c, side] = begin(
                remote(
                    partial[a].at[origin, far, :, cols[side]],
                    far_in[side].at[a, step, c],
                    far_send.at[a, step, c, side],
                    far_recv.at[a, step, c, side],
                    group * SHARDS + target,
                )
            )
        for side, target in enumerate(links):
            near_copies[a, step, c, side, 1] = begin(
                remote(
                    partial[a].at[origin, target, :, cols[side]],
                    near_in.at[a, step, side, :, cols[side]],
                    near_send.at[a, step, c, side, 1],
                    near_recv.at[a, step, c, side, 1],
                    group * SHARDS + target,
                )
            )

    def merge(a, step, c):
        origin = (group + step) % experts_n
        cols = columns(c)
        for side in range(2):
            target = links[1 - side]
            far_copies[a, step, c, side].wait_recv()
            block = far_in[side].at[a, step, c]
            add_into(block, (block, partial[a].at[origin, target, :, cols[side]]), cols[side].size)
            near_copies[a, step, c, 1 - side, 0] = begin(
                remote(
                    block,
                    near_in.at[a, step, 1 - side, :, cols[side]],
                    near_send.at[a, step, c, 1 - side, 0],
                    near_recv.at[a, step, c, 1 - side, 0],
                    group * SHARDS + target,
                )
            )

    def finish(a, step, c):
        origin = (group + step) % experts_n
        whole = pl.ds(c * width, width)
        for side in range(2):
            for part in range(2):
                near_copies[a, step, c, side, part].wait_recv()
        result = total.at[a, step, :, whole]
        add_into(
            result,
            (
                near_in.at[a, step, 0, :, whole],
                near_in.at[a, step, 1, :, whole],
                partial[a].at[origin, shard, :, whole],
            ),
            width,
        )
        out_copies[a, step, c] = begin(
            remote(
                result,
                summed[a].at[group, :, whole],
                out_send.at[a, step, c],
                out_recv.at[a, step, c],
                origin * SHARDS + shard,
                shifts[a],
            )
        )

    for item in order[:WINDOW]:
        send(*item)
    for i, item in enumerate(order):
        merge(*item)
        if i + WINDOW < len(order):
            send(*order[i + WINDOW])
        if i > 0:
            finish(*order[i - 1])
    finish(*order[-1])
    for copy in out_copies.values():
        copy.wait_recv()
    for copy in started:
        copy.wait_send()


def return_call(rows, weights, experts_n, shifts):
    arrays = len(shifts)
    features = weights[0].shape[0]
    capacity = rows[0].shape[0] // (experts_n * SHARDS)
    if capacity % 8 != 0:
        rows = [value.reshape(experts_n * SHARDS, capacity, -1) for value in rows]
    dma = pltpu.SemaphoreType.DMA
    shape = jax.ShapeDtypeStruct((experts_n, capacity, features), jnp.bfloat16)
    first, second = pieces(features // CHUNKS, experts_n)
    return pl.pallas_call(
        functools.partial(return_kernel, experts_n, shifts),
        out_shape=[shape] * arrays,
        in_specs=[pl.BlockSpec(memory_space=pltpu.VMEM)] * 6,
        out_specs=[pl.BlockSpec(memory_space=pl.ANY)] * arrays,
        scratch_shapes=[
            pltpu.VMEM((arrays, experts_n, SHARDS, capacity, features), jnp.bfloat16),
            pltpu.VMEM((arrays, experts_n, CHUNKS, capacity, first.size), jnp.bfloat16),
            pltpu.VMEM((arrays, experts_n, CHUNKS, capacity, second.size), jnp.bfloat16),
            pltpu.VMEM((arrays, experts_n, 2, capacity, features), jnp.bfloat16),
            pltpu.VMEM((arrays, experts_n, capacity, features), jnp.bfloat16),
            dma((arrays, experts_n, CHUNKS, 2)),
            dma((arrays, experts_n, CHUNKS, 2)),
            dma((arrays, experts_n, CHUNKS, 2, 2)),
            dma((arrays, experts_n, CHUNKS, 2, 2)),
            dma((arrays, experts_n, CHUNKS)),
            dma((arrays, experts_n, CHUNKS)),
        ],
        compiler_params=pltpu.CompilerParams(
            collective_id=1, has_side_effects=True, vmem_limit_bytes=VMEM_BYTES
        ),
        name="sums_to_tokens",
    )(*rows, *weights)


def local(
    acts_fwd,
    routes_fwd,
    gates_fwd,
    stash_bwd,
    grads_bwd,
    routes_bwd,
    gates_bwd,
    gain,
    w_gate,
    w_up,
    w_down,
):
    devices = lax.axis_size("expert")
    experts_n = devices // SHARDS
    tok_rows, features = acts_fwd.shape[1:]
    capacity = min(tok_rows, 9 * tok_rows * TOP // (8 * experts_n))
    gate_cols = w_gate[0]
    up_cols = w_up[0]
    down_rows = w_down[0]
    gain_row = gain[0]
    entering = acts_fwd[0]
    select_fwd, unused_gate = slot_tables(routes_fwd[0], gates_fwd[0], experts_n, capacity)
    rows_fwd = pick(select_fwd, normed(entering, gain_row).astype(jnp.bfloat16)).astype(jnp.bfloat16)
    stashed = stash_bwd[0]
    upstream = grads_bwd[0]
    select_bwd, slot_gate = slot_tables(routes_bwd[0], gates_bwd[0], experts_n, capacity)
    rows_bwd = pick(select_bwd, normed(stashed, gain_row).astype(jnp.bfloat16)).astype(jnp.bfloat16)
    rows_grad = (pick(select_bwd, upstream) * slot_gate[:, None]).astype(jnp.bfloat16)
    packed = [
        rows.reshape(experts_n, capacity, features) for rows in (rows_fwd, rows_bwd, rows_grad)
    ]
    wide = -(-experts_n * capacity // 128) * 128

    def token_table(select):
        return jnp.pad(select.T, ((0, 0), (0, wide - experts_n * capacity)))

    passed = (
        (acts_fwd, 1),
        (token_table(select_fwd), 1),
        (jnp.broadcast_to(gates_fwd[0], (tok_rows, 128)), 1),
        (stash_bwd, -1),
        (grads_bwd, -1),
        (token_table(select_bwd), -1),
        (gain.reshape(features // 128, 128), -1),
    )
    gathered, arrived = outward_call(
        packed, [value for value, by in passed], tuple(by for value, by in passed)
    )
    all_fwd, all_bwd, all_grad = [rows.reshape(-1, features) for rows in gathered]
    hidden = expert_forward(all_fwd, gate_cols, up_cols)
    grad_gate, grad_up = expert_backward(all_bwd, all_grad, gate_cols, up_cols, down_rows)
    sums = return_call(
        (hidden, grad_gate, grad_up), (gate_cols, up_cols, down_rows), experts_n, (1, -1)
    )
    back_fwd, back_bwd = [rows.reshape(-1, features) for rows in sums]
    acts, table_fwd, gates, stash, grads, table_bwd, gain_there = arrived
    filled = experts_n * capacity
    mixture = gates[:, :1] * pick(table_fwd[:, :filled], back_fwd)
    layer_out = (acts[0].astype(jnp.float32) + mixture).astype(jnp.bfloat16)
    grad_normed = pick(table_bwd[:, :filled], back_bwd)
    gain_row = gain_there.reshape(features)

    def norm_only(values):
        return normed(values, gain_row)

    unused, pullback = jax.vjp(norm_only, stash[0].astype(jnp.float32))
    grad_input = (grads[0].astype(jnp.float32) + pullback(grad_normed)[0]).astype(jnp.bfloat16)
    return (layer_out[None], grad_input[None])


def solution(mesh):
    return jax.shard_map(
        local,
        mesh=mesh,
        in_specs=(
            P("section", "expert", None),
            P("section", "expert", None),
            P("section", "expert", None),
            P("section", "expert", None),
            P("section", "expert", None),
            P("section", "expert", None),
            P("section", "expert", None),
            P("section", None),
            P("section", None, "expert"),
            P("section", None, "expert"),
            P("section", "expert", None),
        ),
        out_specs=(P("section", "expert", None), P("section", "expert", None)),
        check_vma=False,
    )
```
